32 devices in a mesh: rows: 16 (over z, y, x), feat: 2 (over core).
Axes of the slice: x: 2, y: 2, z: 4, core: 2. Of those that a mesh axis runs over, the one named last changes fastest.
Arguments:
- score: float32 [32768, 128], P('rows', 'feat'), may hold values from -4 to 4
- event: int32 [32768, 128], P('rows', 'feat'), may hold values 0 or 1
- leaf: int32 [32768, 128], P('rows', 'feat'), may hold values from 0 to 1
- bins: int32 [32768, 256], P('rows'), may hold values from 0 to 31
- split_feature: int32 [128], P('feat'), may hold values from 0 to 255
- split_bin: int32 [128], P('feat'), may hold values from 0 to 30
Outputs:
- grad_hist: float32 [256, 32, 2, 128], P(('rows', 'feat'))
- hess_hist: float32 [256, 32, 2, 128], P(('rows', 'feat'))
- new_leaf: int32 [32768, 128], P('rows', 'feat')
The draws below stay inside these ranges and needn't reach their ends.
All inputs are finite; a program needn't handle non-finite values. No bound on the sum of `event` on one device may be relied on, other than what follows from the above.
Results may differ from the reference program's by a relative error of at most 0.0026.
Values may be sent and summed in bfloat16 or wider, within the bound.
A program may use at most 64 MiB of HBM per device.

```python
import jax
import jax.numpy as jnp
from jax import lax

ENDPOINTS = 128
FEATURES = 256
BINS = 32
LEAVES = 2
SAMPLES = 32768


def draw_score(key, part):
    key_noise = jax.random.fold_in(jax.random.fold_in(key, 7), 0)
    position = jnp.arange(SAMPLES, dtype=jnp.float32)[:, None] / SAMPLES
    jitter = 0.7 * jax.random.normal(key_noise, (SAMPLES, ENDPOINTS), jnp.float32)
    trend_rate = 1.1 * jnp.ones((1, ENDPOINTS), jnp.float32)
    return jnp.clip(jitter + trend_rate * (position - 0.5), -4.0, 4.0)


def set_ends(entries, rng, low, largest):
    longest = entries.shape.index(max(entries.shape))
    spots = []
    for shift in (0, 1):
        where = [jax.random.randint(jax.random.fold_in(rng, axis), (), 0, length) for axis, length in enumerate(entries.shape)]
        where[longest] = (where[longest] + shift) % entries.shape[longest]
        spots.append(tuple(where))
    return entries.at[spots[0]].set(low).at[spots[1]].set(largest)


def setup_inputs(seed: int = 0) -> dict:
    key_list = jax.random.split(jax.random.key(seed), 7)
    score = draw_score(jax.random.fold_in(key_list[6], 71), 0)
    event = set_ends((jax.random.randint(key_list[1], (SAMPLES, ENDPOINTS), 0, 4) < 1).astype(jnp.int32), jax.random.fold_in(key_list[1], 1), 0, 1)
    leaf = set_ends(jax.random.randint(key_list[2], (SAMPLES, ENDPOINTS), 0, LEAVES), jax.random.fold_in(key_list[2], 1), 0, LEAVES - 1).astype(jnp.int32)
    bins = set_ends(jax.random.randint(key_list[3], (SAMPLES, FEATURES), 0, BINS), jax.random.fold_in(key_list[3], 1), 0, BINS - 1).astype(jnp.int32)
    split_feature = set_ends(jax.random.randint(key_list[4], (ENDPOINTS,), 0, FEATURES), jax.random.fold_in(key_list[4], 1), 0, FEATURES - 1).astype(jnp.int32)
    split_bin = set_ends(jax.random.randint(key_list[5], (ENDPOINTS,), 0, BINS - 1), jax.random.fold_in(key_list[5], 1), 0, (BINS - 1) - 1).astype(jnp.int32)
    return {"score": score, "event": event, "leaf": leaf, "bins": bins, "split_feature": split_feature, "split_bin": split_bin}


def reference(score, event, leaf, bins, split_feature, split_bin):
    exp_score = jnp.exp(score)
    risk_sum = jnp.cumsum(exp_score[::-1], axis=0)[::-1]
    event_mass = event.astype(jnp.float32)
    event_share = event_mass / risk_sum
    cum_hazard = jnp.cumsum(event_share, axis=0)
    cum_square = jnp.cumsum(event_share / risk_sum, axis=0)
    scale_factor = BINS * LEAVES / SAMPLES
    gradient = scale_factor * (exp_score * cum_hazard - event_mass)
    hessian = scale_factor * (exp_score * cum_hazard - exp_score * exp_score * cum_square)
    in_leaf = leaf[:, None, :] == jnp.arange(LEAVES, dtype=jnp.int32)[None, :, None]
    leaf_weights = jnp.stack([jnp.where(in_leaf, gradient[:, None, :], jnp.zeros((), jnp.float32)),
                              jnp.where(in_leaf, hessian[:, None, :], jnp.zeros((), jnp.float32))], axis=1).astype(jnp.bfloat16)
    flat_weights = leaf_weights.reshape(SAMPLES, 2 * LEAVES * ENDPOINTS).astype(jnp.float32)

    def feature_hist(column):
        return jax.ops.segment_sum(flat_weights, column, num_segments=BINS)

    histograms = lax.map(feature_hist, bins.T).reshape(FEATURES, BINS, 2, LEAVES, ENDPOINTS)
    split_value = jnp.take(bins, split_feature, axis=1)
    new_leaf = 2 * leaf + (split_value > split_bin[None, :]).astype(jnp.int32)
    return histograms[:, :, 0], histograms[:, :, 1], new_leaf
```

```python
import functools

import jax
import jax.numpy as jnp
from jax import lax
from jax.experimental import pallas as pl
from jax.experimental.pallas import tpu as pltpu
from jax.sharding import PartitionSpec as P

BINS = 32
LEAVES = 2
MESH = pl.DeviceIdType.MESH
GROUP = 16
CODE = 32750.0 / (BINS * LEAVES * (1 + 1 / 32)) ** 0.25


def encode(x):
    size = jnp.maximum(jnp.abs(x), 1e-30)
    code = (lax.rsqrt(lax.rsqrt(size)) * CODE + 0.5).astype(jnp.int32)
    return jnp.where(x < 0, -code, code).astype(jnp.int16)


def decode(q):
    v = q.astype(jnp.int32).astype(jnp.float32) * (1.0 / CODE)
    return (v * v) * (v * jnp.abs(v))


def split_dot(tri, x):
    high = x.astype(jnp.bfloat16)
    low = (x - high.astype(jnp.float32)).astype(jnp.bfloat16)
    both = jnp.dot(tri, jnp.concatenate([high, low], axis=1), preferred_element_type=jnp.float32)
    return both[:, : x.shape[1]] + both[:, x.shape[1] :]


def kernel(
    R, U, score, event, leaf, bins, sf, sb,
    new_leaf, gout, hout,
    exp_s, risk_s, cum_s, bins_t, w_s, tile, gat, part, h1, r1, h2, r2, h3, r3, fin, sib,
    sA, rA, s1, q1, s2, q2, s3, q3, s4, q4,
):
    rows, EL = score.shape
    F = bins.shape[1]
    FPC = F // R
    UF = FPC // U
    UR = UF * BINS
    Z = R // 4
    HZ = Z * UR
    DP = GROUP // UF
    STEP = GROUP * BINS
    T = (R // 2) // DP
    TB = min(rows, 256)
    me = lax.axis_index("rows")
    c = lax.axis_index("feat")

    barrier = pltpu.get_barrier_semaphore()

    @pl.loop(1, R)
    def _(k):
        pl.semaphore_signal(barrier, inc=1, device_id={"rows": lax.rem(me + k, R)}, device_id_type=MESH)

    pl.semaphore_signal(barrier, inc=1, device_id={"feat": 1 - c}, device_id_type=MESH)

    ri = lax.broadcasted_iota(jnp.int32, (TB, TB), 0)
    ci = lax.broadcasted_iota(jnp.int32, (TB, TB), 1)
    low_half = lax.broadcasted_iota(jnp.int32, (TB, 2 * EL), 1) < EL

    def twice(x):
        return jnp.concatenate([x, x], axis=1)

    upper = jnp.where(ci >= ri, 1.0, 0.0).astype(jnp.bfloat16)
    carry = jnp.zeros((1, 2 * EL), jnp.float32)
    for b in reversed(range(rows // TB)):
        at = slice(b * TB, (b + 1) * TB)
        e = jnp.exp(twice(score[at, :]))
        exp_s[at, :] = e
        suffix = split_dot(upper, e) + carry
        risk_s[at, :] = suffix
        carry = suffix[0:1, :]
    tile[0] = jnp.broadcast_to(carry, (8, 2 * EL))

    pl.semaphore_wait(barrier, R)

    def total_copy(phase, k):
        return pltpu.make_async_remote_copy(
            src_ref=tile.at[phase], dst_ref=gat.at[phase, k - 1],
            send_sem=sA.at[phase, k - 1], recv_sem=rA.at[phase, k - 1],
            device_id={"rows": lax.rem(me + k, R)}, device_id_type=MESH,
        )

    @pl.loop(1, R)
    def _(k):
        total_copy(0, k).start()

    bins_t[...] = bins[...].astype(jnp.float32).T
    pick = jnp.where(lax.broadcasted_iota(jnp.int32, (F, EL), 0) == sf[...], 1.0, 0.0).astype(jnp.bfloat16)
    value = jnp.dot(
        bins[...].astype(jnp.float32).astype(jnp.bfloat16), pick, preferred_element_type=jnp.float32
    )
    new_leaf[...] = 2 * leaf[...] + jnp.where(value > sb[...].astype(jnp.float32), 1, 0)

    def gathered(phase, later):
        @pl.loop(1, R)
        def _(k):
            total_copy(phase, k).wait()

        def add(k, acc):
            wanted = (k > me) if later else (k <= me)
            return acc + jnp.where(wanted, gat[phase, k - 1], 0.0)

        return lax.fori_loop(1, R, add, jnp.zeros((8, 2 * EL), jnp.float32))[0:1, :]

    later_sum = gathered(0, True)

    lower = jnp.where(ci <= ri, 1.0, 0.0).astype(jnp.bfloat16)
    carry = jnp.zeros((1, 2 * EL), jnp.float32)
    for b in range(rows // TB):
        at = slice(b * TB, (b + 1) * TB)
        risk = risk_s[at, :] + later_sum
        share = twice(event[at, :]).astype(jnp.float32) / risk
        share = jnp.where(low_half, share, share / risk)
        prefix = split_dot(lower, share) + carry
        cum_s[at, :] = prefix
        carry = prefix[TB - 1 : TB, :]
    tile[1] = jnp.broadcast_to(carry, (8, 2 * EL))

    @pl.loop(1, R)
    def _(k):
        total_copy(1, k).start()

    earlier_sum = gathered(1, False)
    scale = BINS * LEAVES / (rows * R)
    for b in range(rows // TB):
        at = slice(b * TB, (b + 1) * TB)
        e = exp_s[at, :]
        p = e * (cum_s[at, :] + earlier_sum)
        p = jnp.where(low_half, p, e * p)
        turned = pltpu.roll(p, EL, 1)
        ev = twice(event[at, :]).astype(jnp.float32)
        grad_hess = scale * jnp.where(low_half, p - ev, turned - p)
        leaves = twice(leaf[at, :])
        for l in range(LEAVES):
            w_s[at, l * 2 * EL : (l + 1) * 2 * EL] = jnp.where(leaves == l, grad_hess, 0.0).astype(jnp.bfloat16)

    level = lax.broadcasted_iota(jnp.int32, (BINS, rows), 0).astype(jnp.float32).astype(jnp.bfloat16)

    def digits(u):
        par = lax.rem(u, 2)
        w1, w2 = 1 + par, 2 - par
        m1 = lax.rem(me // w1, 2)
        m2 = lax.rem(me // w2, 2)
        return w1, w2, m1, m2, me + w1 * (1 - 2 * m1), me + w2 * (1 - 2 * m2)

    def hist(u, t, d1, w1, w2):
        pieces = []
        for i in range(DP):
            spot = t * DP + i
            chip = 4 * lax.rem(spot, Z) + w2 * (spot // Z) + w1 * d1
            for j in range(UF):
                row = bins_t[pl.ds(chip * FPC + u * UF + j, 1), :].astype(jnp.bfloat16)
                hit = jnp.broadcast_to(row, (BINS, rows)) == level
                pieces.append(jnp.where(hit, jnp.bfloat16(1), jnp.bfloat16(0)))
        return jnp.dot(jnp.concatenate(pieces, axis=0), w_s[...], preferred_element_type=jnp.float32)

    def copy1(u):
        p1 = digits(u)[4]
        return pltpu.make_async_remote_copy(
            src_ref=h1.at[u], dst_ref=r1.at[u], send_sem=s1.at[u], recv_sem=q1.at[u],
            device_id={"rows": p1}, device_id_type=MESH,
        )

    def copy2(u):
        p2 = digits(u)[5]
        return pltpu.make_async_remote_copy(
            src_ref=h2.at[u], dst_ref=r2.at[u], send_sem=s2.at[u], recv_sem=q2.at[u],
            device_id={"rows": p2}, device_id_type=MESH,
        )

    mz = me // 4

    def copy3(u, k):
        return pltpu.make_async_remote_copy(
            src_ref=h3.at[u, k - 1], dst_ref=r3.at[u, k - 1],
            send_sem=s3.at[u, k - 1], recv_sem=q3.at[u, k - 1],
            device_id={"rows": 4 * lax.rem(mz + k, Z) + lax.rem(me, 4)}, device_id_type=MESH,
        )

    @pl.loop(0, U)
    def _(u):
        w1, w2, m1, *_ = digits(u)

        @pl.loop(0, T)
        def _(t):
            h1[u, pl.ds(pl.multiple_of(t * STEP, STEP), STEP), :] = encode(hist(u, t, 1 - m1, w1, w2))

        copy1(u).start()

    @pl.loop(0, U)
    def _(u):
        w1, w2, m1, *_ = digits(u)

        @pl.loop(0, T)
        def _(t):
            part[u, pl.ds(pl.multiple_of(t * STEP, STEP), STEP), :] = hist(u, t, m1, w1, w2)

    def second(u):
        m2 = digits(u)[3]
        copy1(u).wait_recv()
        away = pl.ds(pl.multiple_of((1 - m2) * HZ, HZ), HZ)
        h2[u] = encode(part[u, away, :] + decode(r1[u, away, :]))
        copy2(u).start()

    def third(u):
        m2 = digits(u)[3]
        copy2(u).wait_recv()

        def sums(z):
            near = pl.ds(pl.multiple_of(m2 * HZ + z * UR, UR), UR)
            there = pl.ds(pl.multiple_of(z * UR, UR), UR)
            return part[u, near, :] + decode(r1[u, near, :]) + decode(r2[u, there, :])

        @pl.loop(1, Z)
        def _(k):
            h3[u, k - 1] = encode(sums(lax.rem(mz + k, Z)))
            copy3(u, k).start()

        fin[u] = sums(mz)

    lag = min(2, U)

    @pl.loop(0, U + lag)
    def _(t):
        @pl.when(t < U)
        def _():
            second(t)

        @pl.when(t >= lag)
        def _():
            third(t - lag)

    @pl.loop(0, U)
    def _(u):
        @pl.loop(1, Z)
        def _(k):
            copy3(u, k).wait_recv()
            fin[u] = fin[u] + decode(r3[u, k - 1])

    half = U // 2
    swap = pltpu.make_async_remote_copy(
        src_ref=fin.at[pl.ds((1 - c) * half, half)], dst_ref=sib, send_sem=s4, recv_sem=q4,
        device_id={"feat": 1 - c}, device_id_type=MESH,
    )
    swap.start()

    @pl.loop(0, U)
    def _(u):
        copy1(u).wait_send()
        copy2(u).wait_send()

        @pl.loop(1, Z)
        def _(k):
            copy3(u, k).wait_send()

    swap.wait()
    lanes = lax.broadcasted_iota(jnp.int32, (UR, 2 * EL), 1) < EL
    for v in range(half):
        at = slice(v * UR, (v + 1) * UR)
        own, other = fin[c * half + v], sib[v]
        first = jnp.where(c == 0, own, other)
        last = jnp.where(c == 0, other, own)
        for l in range(LEAVES):
            a, z = (y[:, l * 2 * EL : (l + 1) * 2 * EL] for y in (first, last))
            gout[at, l, :] = jnp.where(lanes, a, pltpu.roll(z, EL, 1))
            hout[at, l, :] = jnp.where(lanes, pltpu.roll(a, EL, 1), z)


def per_device(R, score, event, leaf, bins, split_feature, split_bin):
    rows, EL = score.shape
    F = bins.shape[1]
    FPC = F // R
    U = min(8, FPC)
    UR = FPC // U * BINS
    Z = R // 4
    C = LEAVES * 2 * EL
    own = FPC // 2 * BINS
    f32, i16 = jnp.float32, jnp.int16
    dma = pltpu.SemaphoreType.DMA
    new_leaf, grad, hess = pl.pallas_call(
        functools.partial(kernel, R, U),
        out_shape=(
            jax.ShapeDtypeStruct((rows, EL), jnp.int32),
            jax.ShapeDtypeStruct((own, LEAVES, 2 * EL), f32),
            jax.ShapeDtypeStruct((own, LEAVES, 2 * EL), f32),
        ),
        in_specs=[pl.BlockSpec(memory_space=pltpu.VMEM)] * 6,
        out_specs=[pl.BlockSpec(memory_space=pltpu.VMEM)] * 3,
        scratch_shapes=[
            pltpu.VMEM((rows, 2 * EL), f32),
            pltpu.VMEM((rows, 2 * EL), f32),
            pltpu.VMEM((rows, 2 * EL), f32),
            pltpu.VMEM((F, rows), f32),
            pltpu.VMEM((rows, C), jnp.bfloat16),
            pltpu.VMEM((2, 8, 2 * EL), f32),
            pltpu.VMEM((2, R - 1, 8, 2 * EL), f32),
            pltpu.VMEM((U, R // 2 * UR, C), f32),
            pltpu.VMEM((U, R // 2 * UR, C), i16),
            pltpu.VMEM((U, R // 2 * UR, C), i16),
            pltpu.VMEM((U, Z * UR, C), i16),
            pltpu.VMEM((U, Z * UR, C), i16),
            pltpu.VMEM((U, Z - 1, UR, C), i16),
            pltpu.VMEM((U, Z - 1, UR, C), i16),
            pltpu.VMEM((U, UR, C), f32),
            pltpu.VMEM((U // 2, UR, C), f32),
            dma((2, R - 1)), dma((2, R - 1)),
            dma((U,)), dma((U,)), dma((U,)), dma((U,)),
            dma((U, Z - 1)), dma((U, Z - 1)),
            dma, dma,
        ],
        compiler_params=pltpu.CompilerParams(
            collective_id=0, has_side_effects=True, vmem_limit_bytes=52 * 2**20
        ),
        cost_estimate=pl.CostEstimate(
            flops=2 * F * BINS * rows * C, bytes_accessed=4 * rows * F, transcendentals=rows * EL
        ),
    )(score, event, leaf, bins, split_feature[None, :], split_bin[None, :])
    shape = (own // BINS, BINS, LEAVES, 2 * EL)
    return grad.reshape(shape), hess.reshape(shape), new_leaf


def solution(mesh):
    return jax.shard_map(
        functools.partial(per_device, mesh.shape["rows"]),
        mesh=mesh,
        in_specs=(
            P("rows", "feat"),
            P("rows", "feat"),
            P("rows", "feat"),
            P("rows", None),
            P("feat"),
            P("feat"),
        ),
        out_specs=(
            P(("rows", "feat"), None, None, None),
            P(("rows", "feat"), None, None, None),
            P("rows", "feat"),
        ),
        check_vma=False,
    )
```

```python
import functools

import jax
import jax.numpy as jnp
from jax import lax
from jax.experimental import pallas as pl
from jax.experimental.pallas import tpu as pltpu
from jax.sharding import PartitionSpec as P

BINS = 32
LEAVES = 2
MESH = pl.DeviceIdType.MESH
GROUP = 16
CODE = 32750.0 / (BINS * LEAVES * (1 + 1 / 32)) ** 0.25


def encode(x):
    size = jnp.maximum(jnp.abs(x), 1e-30)
    code = (lax.rsqrt(lax.rsqrt(size)) * CODE + 0.5).astype(jnp.int32)
    return jnp.where(x < 0, -code, code).astype(jnp.int16)


def decode(q):
    v = q.astype(jnp.int32).astype(jnp.float32) * (1.0 / CODE)
    return (v * v) * (v * jnp.abs(v))


def split_dot(tri, x):
    high = x.astype(jnp.bfloat16)
    low = (x - high.astype(jnp.float32)).astype(jnp.bfloat16)
    both = jnp.dot(tri, jnp.concatenate([high, low], axis=1), preferred_element_type=jnp.float32)
    return both[:, : x.shape[1]] + both[:, x.shape[1] :]


def kernel(
    R, U, score, event, leaf, bins, sf, sb,
    new_leaf, gout, hout,
    exp_s, risk_s, cum_s, event_s, leaf_s, bins_t, w_s, tile, gat, part, h1, r1, h2, r2, h3, r3, fin, sib,
    sA, rA, s1, q1, s2, q2, s3, q3, s4, q4,
):
    EL, rows = score.shape
    F = bins.shape[1]
    FPC = F // R
    UF = FPC // U
    UR = UF * BINS
    Z = R // 4
    HZ = Z * UR
    DP = GROUP // UF
    STEP = GROUP * BINS
    T = (R // 2) // DP
    TB = min(rows, 256)
    me = lax.axis_index("rows")
    c = lax.axis_index("feat")

    barrier = pltpu.get_barrier_semaphore()

    @pl.loop(1, R)
    def _(k):
        pl.semaphore_signal(barrier, inc=1, device_id={"rows": lax.rem(me + k, R)}, device_id_type=MESH)

    pl.semaphore_signal(barrier, inc=1, device_id={"feat": 1 - c}, device_id_type=MESH)

    ri = lax.broadcasted_iota(jnp.int32, (TB, TB), 0)
    ci = lax.broadcasted_iota(jnp.int32, (TB, TB), 1)
    low_half = lax.broadcasted_iota(jnp.int32, (TB, 2 * EL), 1) < EL

    def twice(x):
        return jnp.concatenate([x, x], axis=0).T

    upper = jnp.where(ci >= ri, 1.0, 0.0).astype(jnp.bfloat16)
    carry = jnp.zeros((1, 2 * EL), jnp.float32)
    for b in reversed(range(rows // TB)):
        at = slice(b * TB, (b + 1) * TB)
        e = jnp.exp(twice(score[:, at]))
        exp_s[at, :] = e
        suffix = split_dot(upper, e) + carry
        risk_s[at, :] = suffix
        carry = suffix[0:1, :]
    tile[0] = jnp.broadcast_to(carry, (8, 2 * EL))

    pl.semaphore_wait(barrier, R)

    def total_copy(phase, k):
        return pltpu.make_async_remote_copy(
            src_ref=tile.at[phase], dst_ref=gat.at[phase, k - 1],
            send_sem=sA.at[phase, k - 1], recv_sem=rA.at[phase, k - 1],
            device_id={"rows": lax.rem(me + k, R)}, device_id_type=MESH,
        )

    @pl.loop(1, R)
    def _(k):
        total_copy(0, k).start()

    for b in range(rows // TB):
        at = slice(b * TB, (b + 1) * TB)
        event_s[at, :] = twice(event[:, at].astype(jnp.float32))
        leaf_s[at, :] = twice(leaf[:, at].astype(jnp.float32))

    def gathered(phase, later):
        @pl.loop(1, R)
        def _(k):
            total_copy(phase, k).wait()

        def add(k, acc):
            wanted = (k > me) if later else (k <= me)
            return acc + jnp.where(wanted, gat[phase, k - 1], 0.0)

        return lax.fori_loop(1, R, add, jnp.zeros((8, 2 * EL), jnp.float32))[0:1, :]

    later_sum = gathered(0, True)

    lower = jnp.where(ci <= ri, 1.0, 0.0).astype(jnp.bfloat16)
    carry = jnp.zeros((1, 2 * EL), jnp.float32)
    for b in range(rows // TB):
        at = slice(b * TB, (b + 1) * TB)
        risk = risk_s[at, :] + later_sum
        share = event_s[at, :] / risk
        share = jnp.where(low_half, share, share / risk)
        prefix = split_dot(lower, share) + carry
        cum_s[at, :] = prefix
        carry = prefix[TB - 1 : TB, :]
    tile[1] = jnp.broadcast_to(carry, (8, 2 * EL))

    @pl.loop(1, R)
    def _(k):
        total_copy(1, k).start()

    bins_t[...] = bins[...].astype(jnp.float32).T
    ids = lax.broadcasted_iota(jnp.int32, (EL, F), 1).astype(jnp.float32)
    wanted = jnp.broadcast_to(sf[...].astype(jnp.float32), (F, EL)).T
    pick = jnp.where(ids == wanted, 1.0, 0.0).astype(jnp.bfloat16)
    limit = jnp.broadcast_to(sb[...].astype(jnp.float32), (F, EL)).T[:, 0:1]
    value = jnp.dot(pick, bins_t[...].astype(jnp.bfloat16), preferred_element_type=jnp.float32)
    new_leaf[...] = 2 * leaf[...] + jnp.where(value > limit, 1, 0)

    earlier_sum = gathered(1, False)
    scale = BINS * LEAVES / (rows * R)
    for b in range(rows // TB):
        at = slice(b * TB, (b + 1) * TB)
        e = exp_s[at, :]
        p = e * (cum_s[at, :] + earlier_sum)
        p = jnp.where(low_half, p, e * p)
        turned = pltpu.roll(p, EL, 1)
        ev = event_s[at, :]
        grad_hess = scale * jnp.where(low_half, p - ev, turned - p)
        leaves = leaf_s[at, :]
        for l in range(LEAVES):
            w_s[at, l * 2 * EL : (l + 1) * 2 * EL] = jnp.where(leaves == l, grad_hess, 0.0).astype(jnp.bfloat16)

    level = lax.broadcasted_iota(jnp.int32, (BINS, rows), 0).astype(jnp.float32).astype(jnp.bfloat16)

    def digits(u):
        par = lax.rem(u, 2)
        w1, w2 = 1 + par, 2 - par
        m1 = lax.rem(me // w1, 2)
        m2 = lax.rem(me // w2, 2)
        return w1, w2, m1, m2, me + w1 * (1 - 2 * m1), me + w2 * (1 - 2 * m2)

    def hist(u, t, d1, w1, w2):
        pieces = []
        for i in range(DP):
            spot = t * DP + i
            chip = 4 * lax.rem(spot, Z) + w2 * (spot // Z) + w1 * d1
            for j in range(UF):
                row = bins_t[pl.ds(chip * FPC + u * UF + j, 1), :].astype(jnp.bfloat16)
                hit = jnp.broadcast_to(row, (BINS, rows)) == level
                pieces.append(jnp.where(hit, jnp.bfloat16(1), jnp.bfloat16(0)))
        return jnp.dot(jnp.concatenate(pieces, axis=0), w_s[...], preferred_element_type=jnp.float32)

    def copy1(u):
        p1 = digits(u)[4]
        return pltpu.make_async_remote_copy(
            src_ref=h1.at[u], dst_ref=r1.at[u], send_sem=s1.at[u], recv_sem=q1.at[u],
            device_id={"rows": p1}, device_id_type=MESH,
        )

    def copy2(u):
        p2 = digits(u)[5]
        return pltpu.make_async_remote_copy(
            src_ref=h2.at[u], dst_ref=r2.at[u], send_sem=s2.at[u], recv_sem=q2.at[u],
            device_id={"rows": p2}, device_id_type=MESH,
        )

    mz = me // 4

    def copy3(u, k):
        return pltpu.make_async_remote_copy(
            src_ref=h3.at[u, k - 1], dst_ref=r3.at[u, k - 1],
            send_sem=s3.at[u, k - 1], recv_sem=q3.at[u, k - 1],
            device_id={"rows": 4 * lax.rem(mz + k, Z) + lax.rem(me, 4)}, device_id_type=MESH,
        )

    def first(u):
        w1, w2, m1, *_ = digits(u)

        @pl.loop(0, T)
        def _(t):
            h1[u, pl.ds(pl.multiple_of(t * STEP, STEP), STEP), :] = encode(hist(u, t, 1 - m1, w1, w2))

        copy1(u).start()

    def keep(u):
        w1, w2, m1, *_ = digits(u)

        @pl.loop(0, T)
        def _(t):
            part[u, pl.ds(pl.multiple_of(t * STEP, STEP), STEP), :] = hist(u, t, m1, w1, w2)

    def second(u):
        m2 = digits(u)[3]
        copy1(u).wait_recv()
        away = pl.ds(pl.multiple_of((1 - m2) * HZ, HZ), HZ)
        h2[u] = encode(part[u, away, :] + decode(r1[u, away, :]))
        copy2(u).start()

    def third(u):
        m2 = digits(u)[3]
        copy2(u).wait_recv()

        def sums(z):
            near = pl.ds(pl.multiple_of(m2 * HZ + z * UR, UR), UR)
            there = pl.ds(pl.multiple_of(z * UR, UR), UR)
            return part[u, near, :] + decode(r1[u, near, :]) + decode(r2[u, there, :])

        @pl.loop(1, Z)
        def _(k):
            h3[u, k - 1] = encode(sums(lax.rem(mz + k, Z)))
            copy3(u, k).start()

        fin[u] = sums(mz)

    lag = min(4, U)
    lag3 = lag + 2

    @pl.loop(0, U + lag3)
    def _(t):
        @pl.when(t < U)
        def _():
            first(t)

        @pl.when((t >= lag) & (t < U + lag))
        def _():
            keep(t - lag)
            second(t - lag)

        @pl.when(t >= lag3)
        def _():
            third(t - lag3)

    @pl.loop(0, U)
    def _(u):
        @pl.loop(1, Z)
        def _(k):
            copy3(u, k).wait_recv()
            fin[u] = fin[u] + decode(r3[u, k - 1])

    half = U // 2
    swap = pltpu.make_async_remote_copy(
        src_ref=fin.at[pl.ds((1 - c) * half, half)], dst_ref=sib, send_sem=s4, recv_sem=q4,
        device_id={"feat": 1 - c}, device_id_type=MESH,
    )
    swap.start()

    @pl.loop(0, U)
    def _(u):
        copy1(u).wait_send()
        copy2(u).wait_send()

        @pl.loop(1, Z)
        def _(k):
            copy3(u, k).wait_send()

    swap.wait()
    lanes = lax.broadcasted_iota(jnp.int32, (UR, 2 * EL), 1) < EL
    for v in range(half):
        at = slice(v * UR, (v + 1) * UR)
        own, other = fin[c * half + v], sib[v]
        first = jnp.where(c == 0, own, other)
        last = jnp.where(c == 0, other, own)
        for l in range(LEAVES):
            a, z = (y[:, l * 2 * EL : (l + 1) * 2 * EL] for y in (first, last))
            gout[at, l, :] = jnp.where(lanes, a, pltpu.roll(z, EL, 1))
            hout[at, l, :] = jnp.where(lanes, pltpu.roll(a, EL, 1), z)


def per_device(R, score, event, leaf, bins, split_feature, split_bin):
    rows, EL = score.shape
    F = bins.shape[1]
    FPC = F // R
    U = min(8, FPC)
    UR = FPC // U * BINS
    Z = R // 4
    C = LEAVES * 2 * EL
    own = FPC // 2 * BINS
    f32, i16 = jnp.float32, jnp.int16
    dma = pltpu.SemaphoreType.DMA
    new_leaf, grad, hess = pl.pallas_call(
        functools.partial(kernel, R, U),
        out_shape=(
            jax.ShapeDtypeStruct((EL, rows), jnp.int32),
            jax.ShapeDtypeStruct((own, LEAVES, 2 * EL), f32),
            jax.ShapeDtypeStruct((own, LEAVES, 2 * EL), f32),
        ),
        in_specs=[pl.BlockSpec(memory_space=pltpu.VMEM)] * 6,
        out_specs=[pl.BlockSpec(memory_space=pltpu.VMEM)] * 3,
        scratch_shapes=[
            pltpu.VMEM((rows, 2 * EL), f32),
            pltpu.VMEM((rows, 2 * EL), f32),
            pltpu.VMEM((rows, 2 * EL), f32),
            pltpu.VMEM((rows, 2 * EL), f32),
            pltpu.VMEM((rows, 2 * EL), f32),
            pltpu.VMEM((F, rows), f32),
            pltpu.VMEM((rows, C), jnp.bfloat16),
            pltpu.VMEM((2, 8, 2 * EL), f32),
            pltpu.VMEM((2, R - 1, 8, 2 * EL), f32),
            pltpu.VMEM((U, R // 2 * UR, C), f32),
            pltpu.VMEM((U, R // 2 * UR, C), i16),
            pltpu.VMEM((U, R // 2 * UR, C), i16),
            pltpu.VMEM((U, Z * UR, C), i16),
            pltpu.VMEM((U, Z * UR, C), i16),
            pltpu.VMEM((U, Z - 1, UR, C), i16),
            pltpu.VMEM((U, Z - 1, UR, C), i16),
            pltpu.VMEM((U, UR, C), f32),
            pltpu.VMEM((U // 2, UR, C), f32),
            dma((2, R - 1)), dma((2, R - 1)),
            dma((U,)), dma((U,)), dma((U,)), dma((U,)),
            dma((U, Z - 1)), dma((U, Z - 1)),
            dma, dma,
        ],
        compiler_params=pltpu.CompilerParams(
            collective_id=0, has_side_effects=True, vmem_limit_bytes=52 * 2**20
        ),
        cost_estimate=pl.CostEstimate(
            flops=2 * F * BINS * rows * C, bytes_accessed=4 * rows * F, transcendentals=rows * EL
        ),
    )(score.T, event.T, leaf.T, bins, split_feature[None, :], split_bin[None, :])
    shape = (own // BINS, BINS, LEAVES, 2 * EL)
    return grad.reshape(shape), hess.reshape(shape), new_leaf.T


def solution(mesh):
    return jax.shard_map(
        functools.partial(per_device, mesh.shape["rows"]),
        mesh=mesh,
        in_specs=(
            P("rows", "feat"),
            P("rows", "feat"),
            P("rows", "feat"),
            P("rows", None),
            P("feat"),
            P("feat"),
        ),
        out_specs=(
            P(("rows", "feat"), None, None, None),
            P(("rows", "feat"), None, None, None),
            P("rows", "feat"),
        ),
        check_vma=False,
    )
```

```python
import functools

import jax
import jax.numpy as jnp
from jax import lax
from jax.experimental import pallas as pl
from jax.experimental.pallas import tpu as pltpu
from jax.sharding import PartitionSpec as P

BINS = 32
LEAVES = 2
MESH = pl.DeviceIdType.MESH
GROUP = 16
CODE = 32750.0 / (BINS * LEAVES * (1 + 1 / 32)) ** 0.25


def encode(x):
    size = jnp.maximum(jnp.abs(x), 1e-30)
    code = (lax.rsqrt(lax.rsqrt(size)) * CODE + 0.5).astype(jnp.int32)
    return jnp.where(x < 0, -code, code).astype(jnp.int16)


def decode(q):
    v = q.astype(jnp.int32).astype(jnp.float32) * (1.0 / CODE)
    return (v * v) * (v * jnp.abs(v))


def split_dot(tri, x):
    high = x.astype(jnp.bfloat16)
    low = (x - high.astype(jnp.float32)).astype(jnp.bfloat16)
    both = jnp.dot(tri, jnp.concatenate([high, low], axis=1), preferred_element_type=jnp.float32)
    return both[:, : x.shape[1]] + both[:, x.shape[1] :]


def kernel(
    R, U, score, event, leaf, bins, sf, sb,
    new_leaf, gout, hout,
    exp_s, risk_s, cum_s, event_s, leaf_s, bins_t, w_s, tile, gat, part, h1, r1, h2, r2, h3, r3, fin, sib,
    sA, rA, s1, q1, s2, q2, s3, q3, s4, q4,
):
    EL, rows = score.shape
    F = bins.shape[1]
    FPC = F // R
    UF = FPC // U
    UR = UF * BINS
    Z = R // 4
    HZ = Z * UR
    DP = GROUP // UF
    STEP = GROUP * BINS
    T = (R // 2) // DP
    TB = min(rows, 256)
    me = lax.axis_index("rows")
    c = lax.axis_index("feat")

    barrier = pltpu.get_barrier_semaphore()

    @pl.loop(1, R)
    def _(k):
        pl.semaphore_signal(barrier, inc=1, device_id={"rows": lax.rem(me + k, R)}, device_id_type=MESH)

    pl.semaphore_signal(barrier, inc=1, device_id={"feat": 1 - c}, device_id_type=MESH)

    ri = lax.broadcasted_iota(jnp.int32, (TB, TB), 0)
    ci = lax.broadcasted_iota(jnp.int32, (TB, TB), 1)
    low_half = lax.broadcasted_iota(jnp.int32, (TB, 2 * EL), 1) < EL

    def twice(x):
        return jnp.concatenate([x, x], axis=0).T

    upper = jnp.where(ci >= ri, 1.0, 0.0).astype(jnp.bfloat16)
    carry = jnp.zeros((1, 2 * EL), jnp.float32)
    for b in reversed(range(rows // TB)):
        at = slice(b * TB, (b + 1) * TB)
        e = jnp.exp(twice(score[:, at]))
        exp_s[at, :] = e
        suffix = split_dot(upper, e) + carry
        risk_s[at, :] = suffix
        carry = suffix[0:1, :]
    tile[0] = jnp.broadcast_to(carry, (8, 2 * EL))

    pl.semaphore_wait(barrier, R)

    def total_copy(phase, k):
        return pltpu.make_async_remote_copy(
            src_ref=tile.at[phase], dst_ref=gat.at[phase, k - 1],
            send_sem=sA.at[phase, k - 1], recv_sem=rA.at[phase, k - 1],
            device_id={"rows": lax.rem(me + k, R)}, device_id_type=MESH,
        )

    @pl.loop(1, R)
    def _(k):
        total_copy(0, k).start()

    for b in range(rows // TB):
        at = slice(b * TB, (b + 1) * TB)
        event_s[at, :] = twice(event[:, at].astype(jnp.float32))
        leaf_s[at, :] = twice(leaf[:, at].astype(jnp.float32))

    def gathered(phase, later):
        @pl.loop(1, R)
        def _(k):
            total_copy(phase, k).wait_recv()

        def add(k, acc):
            wanted = (k > me) if later else (k <= me)
            return acc + jnp.where(wanted, gat[phase, k - 1], 0.0)

        return lax.fori_loop(1, R, add, jnp.zeros((8, 2 * EL), jnp.float32))[0:1, :]

    later_sum = gathered(0, True)

    lower = jnp.where(ci <= ri, 1.0, 0.0).astype(jnp.bfloat16)
    carry = jnp.zeros((1, 2 * EL), jnp.float32)
    for b in range(rows // TB):
        at = slice(b * TB, (b + 1) * TB)
        risk = risk_s[at, :] + later_sum
        share = event_s[at, :] / risk
        share = jnp.where(low_half, share, share / risk)
        prefix = split_dot(lower, share) + carry
        cum_s[at, :] = prefix
        carry = prefix[TB - 1 : TB, :]
    tile[1] = jnp.broadcast_to(carry, (8, 2 * EL))

    @pl.loop(1, R)
    def _(k):
        total_copy(1, k).start()

    bins_t[...] = bins[...].astype(jnp.float32).T

    earlier_sum = gathered(1, False)
    scale = BINS * LEAVES / (rows * R)
    for b in range(rows // TB):
        at = slice(b * TB, (b + 1) * TB)
        e = exp_s[at, :]
        p = e * (cum_s[at, :] + earlier_sum)
        p = jnp.where(low_half, p, e * p)
        turned = pltpu.roll(p, EL, 1)
        ev = event_s[at, :]
        grad_hess = scale * jnp.where(low_half, p - ev, turned - p)
        leaves = leaf_s[at, :]
        for l in range(LEAVES):
            w_s[at, l * 2 * EL : (l + 1) * 2 * EL] = jnp.where(leaves == l, grad_hess, 0.0).astype(jnp.bfloat16)

    level = lax.broadcasted_iota(jnp.int32, (BINS, rows), 0).astype(jnp.float32).astype(jnp.bfloat16)

    def digits(u):
        par = lax.rem(u, 2)
        w1, w2 = 1 + par, 2 - par
        m1 = lax.rem(me // w1, 2)
        m2 = lax.rem(me // w2, 2)
        return w1, w2, m1, m2, me + w1 * (1 - 2 * m1), me + w2 * (1 - 2 * m2)

    def hist(u, t, d1, w1, w2):
        pieces = []
        for i in range(DP):
            spot = t * DP + i
            chip = 4 * lax.rem(spot, Z) + w2 * (spot // Z) + w1 * d1
            for j in range(UF):
                row = bins_t[pl.ds(chip * FPC + u * UF + j, 1), :].astype(jnp.bfloat16)
                hit = jnp.broadcast_to(row, (BINS, rows)) == level
                pieces.append(jnp.where(hit, jnp.bfloat16(1), jnp.bfloat16(0)))
        return jnp.dot(jnp.concatenate(pieces, axis=0), w_s[...], preferred_element_type=jnp.float32)

    def copy1(u):
        p1 = digits(u)[4]
        return pltpu.make_async_remote_copy(
            src_ref=h1.at[u], dst_ref=r1.at[u], send_sem=s1.at[u], recv_sem=q1.at[u],
            device_id={"rows": p1}, device_id_type=MESH,
        )

    def copy2(u):
        p2 = digits(u)[5]
        return pltpu.make_async_remote_copy(
            src_ref=h2.at[u], dst_ref=r2.at[u], send_sem=s2.at[u], recv_sem=q2.at[u],
            device_id={"rows": p2}, device_id_type=MESH,
        )

    mz = me // 4

    def copy3(u, k):
        return pltpu.make_async_remote_copy(
            src_ref=h3.at[u, k - 1], dst_ref=r3.at[u, k - 1],
            send_sem=s3.at[u, k - 1], recv_sem=q3.at[u, k - 1],
            device_id={"rows": 4 * lax.rem(mz + k, Z) + lax.rem(me, 4)}, device_id_type=MESH,
        )

    def first(u):
        w1, w2, m1, *_ = digits(u)

        @pl.loop(0, T)
        def _(t):
            h1[u, pl.ds(pl.multiple_of(t * STEP, STEP), STEP), :] = encode(hist(u, t, 1 - m1, w1, w2))

        copy1(u).start()

    def keep(u):
        w1, w2, m1, *_ = digits(u)

        @pl.loop(0, T)
        def _(t):
            part[u, pl.ds(pl.multiple_of(t * STEP, STEP), STEP), :] = hist(u, t, m1, w1, w2)

    def second(u):
        m2 = digits(u)[3]
        copy1(u).wait_recv()
        away = pl.ds(pl.multiple_of((1 - m2) * HZ, HZ), HZ)
        h2[u] = encode(part[u, away, :] + decode(r1[u, away, :]))
        copy2(u).start()

    def third(u):
        m2 = digits(u)[3]
        copy2(u).wait_recv()

        def sums(z):
            near = pl.ds(pl.multiple_of(m2 * HZ + z * UR, UR), UR)
            there = pl.ds(pl.multiple_of(z * UR, UR), UR)
            return part[u, near, :] + decode(r1[u, near, :]) + decode(r2[u, there, :])

        @pl.loop(1, Z)
        def _(k):
            h3[u, k - 1] = encode(sums(lax.rem(mz + k, Z)))
            copy3(u, k).start()

        fin[u] = sums(mz)

    lag = min(2, U)
    lag3 = lag + 2

    @pl.loop(0, U + lag3)
    def _(t):
        @pl.when(t < U)
        def _():
            first(t)

        @pl.when((t >= lag) & (t < U + lag))
        def _():
            keep(t - lag)
            second(t - lag)

        @pl.when(t >= lag3)
        def _():
            third(t - lag3)

    ids = lax.broadcasted_iota(jnp.int32, (EL, F), 1).astype(jnp.float32)
    wanted = jnp.broadcast_to(sf[...].astype(jnp.float32), (F, EL)).T
    pick = jnp.where(ids == wanted, 1.0, 0.0).astype(jnp.bfloat16)
    limit = jnp.broadcast_to(sb[...].astype(jnp.float32), (F, EL)).T[:, 0:1]
    value = jnp.dot(pick, bins_t[...].astype(jnp.bfloat16), preferred_element_type=jnp.float32)
    new_leaf[...] = 2 * leaf[...] + jnp.where(value > limit, 1, 0)

    @pl.loop(0, U)
    def _(u):
        @pl.loop(1, Z)
        def _(k):
            copy3(u, k).wait_recv()
            fin[u] = fin[u] + decode(r3[u, k - 1])

    half = U // 2
    swap = pltpu.make_async_remote_copy(
        src_ref=fin.at[pl.ds((1 - c) * half, half)], dst_ref=sib, send_sem=s4, recv_sem=q4,
        device_id={"feat": 1 - c}, device_id_type=MESH,
    )
    swap.start()

    @pl.loop(0, U)
    def _(u):
        copy1(u).wait_send()
        copy2(u).wait_send()

        @pl.loop(1, Z)
        def _(k):
            copy3(u, k).wait_send()

    @pl.loop(1, R)
    def _(k):
        total_copy(0, k).wait_send()
        total_copy(1, k).wait_send()

    swap.wait()
    lanes = lax.broadcasted_iota(jnp.int32, (UR, 2 * EL), 1) < EL
    for v in range(half):
        at = slice(v * UR, (v + 1) * UR)
        own, other = fin[c * half + v], sib[v]
        first = jnp.where(c == 0, own, other)
        last = jnp.where(c == 0, other, own)
        for l in range(LEAVES):
            a, z = (y[:, l * 2 * EL : (l + 1) * 2 * EL] for y in (first, last))
            gout[at, l, :] = jnp.where(lanes, a, pltpu.roll(z, EL, 1))
            hout[at, l, :] = jnp.where(lanes, pltpu.roll(a, EL, 1), z)


def per_device(R, score, event, leaf, bins, split_feature, split_bin):
    rows, EL = score.shape
    F = bins.shape[1]
    FPC = F // R
    U = min(8, FPC)
    UR = FPC // U * BINS
    Z = R // 4
    C = LEAVES * 2 * EL
    own = FPC // 2 * BINS
    f32, i16 = jnp.float32, jnp.int16
    dma = pltpu.SemaphoreType.DMA
    new_leaf, grad, hess = pl.pallas_call(
        functools.partial(kernel, R, U),
        out_shape=(
            jax.ShapeDtypeStruct((EL, rows), jnp.int32),
            jax.ShapeDtypeStruct((own, LEAVES, 2 * EL), f32),
            jax.ShapeDtypeStruct((own, LEAVES, 2 * EL), f32),
        ),
        in_specs=[pl.BlockSpec(memory_space=pltpu.VMEM)] * 6,
        out_specs=[pl.BlockSpec(memory_space=pltpu.VMEM)] * 3,
        scratch_shapes=[
            pltpu.VMEM((rows, 2 * EL), f32),
            pltpu.VMEM((rows, 2 * EL), f32),
            pltpu.VMEM((rows, 2 * EL), f32),
            pltpu.VMEM((rows, 2 * EL), f32),
            pltpu.VMEM((rows, 2 * EL), f32),
            pltpu.VMEM((F, rows), f32),
            pltpu.VMEM((rows, C), jnp.bfloat16),
            pltpu.VMEM((2, 8, 2 * EL), f32),
            pltpu.VMEM((2, R - 1, 8, 2 * EL), f32),
            pltpu.VMEM((U, R // 2 * UR, C), f32),
            pltpu.VMEM((U, R // 2 * UR, C), i16),
            pltpu.VMEM((U, R // 2 * UR, C), i16),
            pltpu.VMEM((U, Z * UR, C), i16),
            pltpu.VMEM((U, Z * UR, C), i16),
            pltpu.VMEM((U, Z - 1, UR, C), i16),
            pltpu.VMEM((U, Z - 1, UR, C), i16),
            pltpu.VMEM((U, UR, C), f32),
            pltpu.VMEM((U // 2, UR, C), f32),
            dma((2, R - 1)), dma((2, R - 1)),
            dma((U,)), dma((U,)), dma((U,)), dma((U,)),
            dma((U, Z - 1)), dma((U, Z - 1)),
            dma, dma,
        ],
        compiler_params=pltpu.CompilerParams(
            collective_id=0, has_side_effects=True, vmem_limit_bytes=52 * 2**20
        ),
        cost_estimate=pl.CostEstimate(
            flops=2 * F * BINS * rows * C, bytes_accessed=4 * rows * F, transcendentals=rows * EL
        ),
    )(score.T, event.T, leaf.T, bins, split_feature[None, :], split_bin[None, :])
    shape = (own // BINS, BINS, LEAVES, 2 * EL)
    return grad.reshape(shape), hess.reshape(shape), new_leaf.T


def solution(mesh):
    return jax.shard_map(
        functools.partial(per_device, mesh.shape["rows"]),
        mesh=mesh,
        in_specs=(
            P("rows", "feat"),
            P("rows", "feat"),
            P("rows", "feat"),
            P("rows", None),
            P("feat"),
            P("feat"),
        ),
        out_specs=(
            P(("rows", "feat"), None, None, None),
            P(("rows", "feat"), None, None, None),
            P("rows", "feat"),
        ),
        check_vma=False,
    )
```
